256 devices in a mesh: win: 4 (over z_lo, core), col: 64 (over z_hi, y, x).
Axes of the slice: x: 4, y: 4, z: 8 (z_hi: 4, z_lo: 2; z = z_hi * 2 + z_lo), core: 2. Of those that a mesh axis runs over, the one named last changes fastest.
Arguments:
- forcing: float32 [8, 256, 2, 192, 256], P('win', 'col'), may hold values from -6 to 6
- coefficients: bfloat16 [8, 256, 192, 512], P('win', 'col'), may hold values from -6 to 6
- legendre: float32 [256, 256, 256], P('col'), may hold values from -0.03125 to 0.03125
- weights: float32 [256], replicated, may hold values from 0.25 to 1
- damping: float32 [192, 256], replicated, may hold values from 0.3 to 1
- mixing: float32 [192, 192], replicated, may hold values from -0.4375 to 0.4375
- points: int32 [256], replicated, may hold values from 64 to 512, as said below
- wavenumbers: int32 [256], replicated, may hold values from 0 to 255, each once
Outputs:
- adjoint_output: float32 [8, 256, 2, 192, 256], P('win', 'col')
The draws below stay inside these ranges and needn't reach their ends.
Inputs may be any that keep to these rules, and one draw needn't show every extreme that they name: 64 to 512 grid points on each latitude; the two latitudes next to the equator have 512. A permutation of the zonal wavenumbers 0 to 255; slot s of the spectral arrays holds wavenumber wavenumbers[s].
All inputs are finite; a program needn't handle non-finite values.
Results may differ from the reference program's by a relative error of at most 0.0003.
Values may be sent and summed in bfloat16 or wider, within the bound.
A program may use at most 128 MiB of HBM per device.

```python
import math
import jax
import jax.numpy as jnp
from jax import lax

LON = 512
STEPS = 2
M = 256
N = 256
LAT = 256
FL = 192
SUB = 8


def draw_points(key, part):
    key = jax.random.fold_in(key, 7)
    latitude = jnp.arange(LAT, dtype=jnp.int32)
    polar = jnp.minimum(latitude, LAT - 1 - latitude)
    extra = jax.random.randint(key, (LAT,), 0, LON // 8 + 1).astype(jnp.int32)
    return jnp.minimum(LON, LON // 8 + extra + 2 * polar * LON // LAT).astype(jnp.int32)


def block_levels(key, shape, shards, least, high):
    gain, own = 1.0, jax.random.fold_in(key, 6)
    for dim, parts in shards:
        steps = jnp.exp(jax.random.uniform(jax.random.fold_in(own, dim), (parts,), jnp.float32, least / len(shards), high / len(shards)))
        gain = gain * jnp.repeat(steps, shape[dim] // parts).reshape([-1 if axis == dim else 1 for axis in range(len(shape))])
    return gain


def normal_values(key, shape, scale, reach, pieces=(), held_as=jnp.bfloat16):
    factor_of = block_levels(key, shape, pieces, -0.22, 0.18) if pieces else 1.0
    entries = jax.random.normal(key, shape, jnp.float32) * scale * factor_of
    return jnp.minimum(jnp.maximum(entries, -reach), reach).astype(held_as)


def setup_inputs(seed: int = 0) -> dict:
    arg_keys = jax.random.split(jax.random.key(seed), 9)
    forcing = normal_values(arg_keys[0], (SUB, M, 2, FL, N), 1.0, 6.0, ((0, 4), (1, 64)), jnp.float32)
    coefficients = normal_values(arg_keys[1], (SUB, LAT, FL, LON), 1.0, 6.0, ((0, 4), (1, 64)))
    legendre = normal_values(arg_keys[2], (M, N, LAT), (M * N // 2) ** -0.5, 0.03125, ((0, 64),), jnp.float32)
    weights = jnp.clip(jnp.exp(jax.random.uniform(arg_keys[3], (LAT,), jnp.float32, math.log(0.25), math.log(1.0))), 0.25, 1.0)
    damping = jnp.clip(jnp.exp(jax.random.uniform(arg_keys[4], (FL, N), jnp.float32, math.log(0.3), math.log(1.0))), 0.3, 1.0)
    mixing = normal_values(arg_keys[5], (FL, FL), FL ** -0.5, 0.4375, (), jnp.float32)
    points = draw_points(jax.random.fold_in(arg_keys[8], 71), 0)
    wavenumbers = jax.random.permutation(arg_keys[7], M).astype(jnp.int32)
    return dict(forcing=forcing, coefficients=coefficients, legendre=legendre, weights=weights, damping=damping, mixing=mixing, points=points, wavenumbers=wavenumbers)


HIGH = lax.Precision.HIGHEST


def fourier_table(count, slots, width):
    along = jnp.arange(width, dtype=jnp.int32)
    phase = (slots[:, None].astype(jnp.int32) * along[None, :]) % count
    angle = (2.0 * math.pi) * phase.astype(jnp.float32) / count.astype(jnp.float32)
    live = (along < count).astype(jnp.float32)[None, :]
    return jnp.stack([jnp.cos(angle) * live, -jnp.sin(angle) * live], axis=1)


def grid_column(four_lat, coef_lat, count, wavenumbers, mixing):
    table = fourier_table(count, wavenumbers, coef_lat.shape[1])
    grid = jnp.einsum("srf,srj->fj", four_lat, table, precision=HIGH)
    forced = coef_lat.astype(jnp.float32) * jnp.einsum("fj,fe->ej", grid, mixing, precision=HIGH)
    return jnp.einsum("ej,srj->sre", forced, table, precision=HIGH)


def adjoint_step(state, coef, masked, weighted, damping, mixing, points, wavenumbers):
    four = jnp.einsum("snl,srfn->lsrf", masked, state, precision=HIGH)

    def column(item):
        return grid_column(item[0], item[1], item[2], wavenumbers, mixing)

    back = lax.map(column, (four, coef, points))
    return damping[None, None] * state + jnp.einsum("snl,lsrf->srfn", weighted, back, precision=HIGH)


def reference(forcing, coefficients, legendre, weights, damping, mixing, points, wavenumbers):
    degree = jnp.arange(N, dtype=jnp.int32)
    masked = legendre * (degree[None, :, None] >= wavenumbers[:, None, None]).astype(jnp.float32)
    weighted = masked * weights[None, None, :]

    def run(item):
        state, coef = item
        for step in range(STEPS):
            state = adjoint_step(state, coef, masked, weighted, damping, mixing, points, wavenumbers)
        return state

    later = lax.map(run, (forcing[1:], coefficients[1:]))
    later = jnp.concatenate([later, jnp.zeros_like(forcing[:1])], axis=0)
    return forcing - later
```

```python
import functools
import math

import jax
import jax.numpy as jnp
from jax import lax
from jax.experimental import pallas as pl
from jax.experimental.pallas import tpu as pltpu
from jax.sharding import PartitionSpec as P

STEPS = 2
SLOTS = 4
COLS = 64
ROWS = 16
LEVELS = 192
SIZE = 256
WIDTH = 512
LANES = 384
PARTS = 3
TOP = 32767.0

f32 = jnp.float32
bf16 = jnp.bfloat16
MESH = pl.DeviceIdType.MESH


def split(values):
    high = values.astype(bf16)
    return high, (values - high.astype(f32)).astype(bf16)


def dot(a, b):
    return lax.dot_general(a, b, (((1,), (0,)), ((), ())), preferred_element_type=f32)


def dot_t(a, b):
    return lax.dot_general(a, b, (((1,), (1,)), ((), ())), preferred_element_type=f32)


def dot3(a_high, a_low, b_high, b_low, product=dot):
    return product(a_high, b_high) + (product(a_high, b_low) + product(a_low, b_high))


def widened(row):
    return jnp.concatenate([row] * PARTS, axis=1)


def kernel(
    forcing, coefs, legendre, weights, damping, mixing, row_numbers, points, numbers,
    out,
    send, recv, send_scale, recv_scale, passed, passed_scale,
    stage, state, fwd_high, fwd_low, inv_high, inv_low, damp, mix_pad, mix_high, mix_low,
    perm, eye, tab_high, tab_low, tabt_high, tabt_low, coef_t, op_high, op_low,
    send_sem, recv_sem, send_scale_sem, recv_scale_sem, pass_sem,
):
    win = lax.axis_index("win")
    col = lax.axis_index("col")
    at_z, at_y, at_x = col // 16, (col // 4) % 4, col % 4

    def partner(k):
        z = (at_z + k // 16) % 4
        y = (at_y + (k // 4) % 4) % 4
        x = (at_x + k % 4) % 4
        return z * 16 + y * 4 + x

    barrier = pltpu.get_barrier_semaphore()

    def greet(k, carry):
        pl.semaphore_signal(barrier, inc=1, device_id=(win, partner(k)), device_id_type=MESH)
        return carry

    lax.fori_loop(1, COLS, greet, 0)

    @pl.when(win > 0)
    def _():
        pl.semaphore_signal(barrier, inc=1, device_id=(win - 1, col), device_id_type=MESH)

    @pl.when(win < 3)
    def _():
        pl.semaphore_signal(barrier, inc=1, device_id=(win + 1, col), device_id_type=MESH)

    def in_order(x):
        return jnp.concatenate([x[0, :128], x[1, :128], x[0, 128:], x[1, 128:]], axis=0)

    def spread(values, row, rows):
        for part in range(PARTS):
            stage[part, pl.ds(row, rows, stride=ROWS), :] = values[:, part * 128:(part + 1) * 128]

    def gathered(row, part):
        return stage[part, pl.ds(row, COLS, stride=ROWS), :]

    def peak(values):
        top = jnp.max(jnp.abs(values), axis=0, keepdims=True)
        return jnp.maximum(jnp.maximum(top[:, :128], top[:, 128:256]), top[:, 256:384])

    def encode(top, buf):
        top = jnp.maximum(top, 1e-30)
        send_scale[buf] = top * (1.0 / TOP)
        inverse = TOP / top

        def one(d, carry):
            for part in range(PARTS):
                code = jnp.round(stage[part, pl.ds(pl.multiple_of(d * ROWS, ROWS), ROWS), :] * inverse)
                send[buf, d, :, part * 128:(part + 1) * 128] = code.astype(jnp.int32).astype(jnp.int16)
            return carry

        lax.fori_loop(0, COLS, one, 0, unroll=4)

    def decode(codes, scales):
        def one(d, carry):
            scale = scales(d)
            for part in range(PARTS):
                code = codes(d, part).astype(jnp.int32).astype(f32)
                stage[part, pl.ds(pl.multiple_of(d * ROWS, ROWS), ROWS), :] = code * scale
            return carry

        lax.fori_loop(0, COLS, one, 0, unroll=4)

    def start(buf):
        def one(k, carry):
            d = partner(k)
            pltpu.make_async_remote_copy(
                src_ref=send_scale.at[buf], dst_ref=recv_scale.at[buf, col],
                send_sem=send_scale_sem.at[buf], recv_sem=recv_scale_sem.at[buf],
                device_id=(win, d), device_id_type=MESH,
            ).start()
            pltpu.make_async_remote_copy(
                src_ref=send.at[buf, d], dst_ref=recv.at[buf, col],
                send_sem=send_sem.at[buf], recv_sem=recv_sem.at[buf],
                device_id=(win, d), device_id_type=MESH,
            ).start()
            return carry

        lax.fori_loop(1, COLS, one, 0)
        recv[buf, col] = send[buf, col]
        recv_scale[buf, col] = send_scale[buf]

    def wait_for(buf, data_sem, scale_sem):
        some = recv.at[buf, pl.ds(0, COLS - 1)]
        pltpu.make_async_copy(some, some, data_sem.at[buf]).wait()
        some = recv_scale.at[buf, pl.ds(0, COLS - 1)]
        pltpu.make_async_copy(some, some, scale_sem.at[buf]).wait()

    def arrive(buf):
        wait_for(buf, recv_sem, recv_scale_sem)
        decode(
            lambda d, part: recv[buf, d, :, part * 128:(part + 1) * 128],
            lambda d: recv_scale[buf, d],
        )

    def sent(buf):
        wait_for(buf, send_sem, send_scale_sem)

    def live(sub):
        return jnp.logical_or(sub > 0, win > 0)

    row = lax.broadcasted_iota(jnp.int32, (SIZE, SIZE), 0)
    lane = lax.broadcasted_iota(jnp.int32, (SIZE, SIZE), 1)
    perm[...] = (row == 4 * (lane % COLS) + lane // COLS).astype(f32).astype(bf16)
    eye[...] = (row == lane).astype(f32).astype(bf16)
    permt = (lane == 4 * (row % COLS) + row // COLS).astype(f32).astype(bf16)

    def masked(s):
        keep = (row >= numbers[col * SLOTS + s]).astype(f32)
        return legendre[s] * keep

    def forward_table(s, carry):
        high, low = split(masked(s))
        fwd_high[s] = dot_t(permt, high).astype(bf16)
        fwd_low[s] = dot_t(permt, low).astype(bf16)
        return carry

    lax.fori_loop(0, SLOTS, forward_table, 0)

    def first(sub, carry):
        @pl.when(live(sub))
        def _():
            def slot(s, top):
                high, low = split(in_order(forcing[sub, s]))
                four = dot3(fwd_high[s], fwd_low[s], high, low, dot_t)
                for q in range(SLOTS):
                    spread(four[q * COLS:(q + 1) * COLS], q * SLOTS + s, COLS)
                return jnp.maximum(top, peak(four))

            encode(lax.fori_loop(0, SLOTS, slot, jnp.zeros((1, 128), f32)), sub)

            @pl.when(sub == jnp.where(win > 0, 0, 1))
            def _():
                pl.semaphore_wait(barrier, COLS - 1 + jnp.where(win > 0, 1, 0) + jnp.where(win < 3, 1, 0))

            start(sub)

        return carry

    lax.fori_loop(0, 2, first, 0)

    def inverse_table(s, carry):
        high, low = split(masked(s) * weights[...])
        inv_high[s] = dot(high, perm[...]).astype(bf16)
        inv_low[s] = dot(low, perm[...]).astype(bf16)
        return carry

    lax.fori_loop(0, SLOTS, inverse_table, 0)

    mix_pad[...] = jnp.zeros((SIZE, SIZE), f32)
    mix_pad[:LEVELS, :LEVELS] = mixing[...]
    high, low = split(mix_pad[...])
    mix_high[...] = high
    mix_low[...] = low

    damp_t = jnp.transpose(jnp.concatenate([damping[...], damping[128:]], axis=0))
    damp[...] = jnp.concatenate([damp_t[:, :128], damp_t[:, :128], damp_t[:, 128:]], axis=1)

    wave = jnp.broadcast_to(row_numbers[...].astype(f32).astype(bf16), (16, SIZE))
    wave = dot(wave, perm[...])[:1]

    def table(q, carry):
        count = points[col * SLOTS + q]
        count_f = jnp.full((1, SIZE), count, jnp.int32).astype(f32)
        part_of = 1.0 / count_f

        def angles(rows, step):
            j = (step * lax.broadcasted_iota(jnp.int32, (rows, SIZE), 0)).astype(f32)
            product = j * wave
            rest = product - jnp.floor(product * part_of) * count_f
            rest = jnp.where(rest < 0.0, rest + count_f, rest)
            rest = jnp.where(rest >= count_f, rest - count_f, rest)
            angle = (2.0 * math.pi) * rest / count_f
            return jnp.cos(angle), jnp.sin(angle)

        cos_a, sin_a = angles(WIDTH // 16, 16)
        cos_b, sin_b = angles(16, 1)
        near = lax.broadcasted_iota(jnp.int32, (16, SIZE), 0)
        for a in range(WIDTH // 16):
            keep = (near + 16 * a < count).astype(f32)
            ca, sa = cos_a[a:a + 1] , sin_a[a:a + 1]
            cos = (ca * cos_b - sa * sin_b) * keep
            sin = (sa * cos_b + ca * sin_b) * keep
            for r, value in ((0, cos), (1, -sin)):
                high, low = split(value)
                tabt_high[q, a * 16:(a + 1) * 16, r * SIZE:(r + 1) * SIZE] = high
                tabt_low[q, a * 16:(a + 1) * 16, r * SIZE:(r + 1) * SIZE] = low
        for r in range(2):
            cut = slice(r * SIZE, (r + 1) * SIZE)
            tab_high[q, cut, :] = dot_t(eye[...], tabt_high[q, :, cut]).astype(bf16)
            tab_low[q, cut, :] = dot_t(eye[...], tabt_low[q, :, cut]).astype(bf16)
        for sub in range(2):
            padded = jnp.concatenate([coefs[sub, q], jnp.zeros((SIZE - LEVELS, WIDTH), bf16)], axis=0)
            for h in range(2):
                cut = slice(h * SIZE, (h + 1) * SIZE)
                coef_t[sub, q, cut, :] = dot_t(eye[...], padded[:, cut]).astype(bf16)
        return carry

    lax.fori_loop(0, SLOTS, table, 0)

    def grid(sub, step):
        arrive(sub)
        if step > 0:
            sent(2 + sub)

        def latitude(q, carry):
            for s in range(SLOTS):
                at = q * SLOTS + s
                last = gathered(at, 2)
                real = jnp.concatenate([gathered(at, 0), last], axis=1)
                imag = jnp.concatenate([gathered(at, 1), pltpu.roll(last, 64, 1)], axis=1)
                for r, value in ((0, real), (1, imag)):
                    high, low = split(value)
                    rows = slice(r * SIZE + s * COLS, r * SIZE + (s + 1) * COLS)
                    op_high[q, rows, :] = high
                    op_low[q, rows, :] = low
            return carry

        lax.fori_loop(0, SLOTS, latitude, 0)

        def latitude(q, top):
            values = dot3(tabt_high[q], tabt_low[q], op_high[q], op_low[q])
            high, low = split(values)
            mixed = dot3(high, low, mix_high[...], mix_low[...])
            high, low = split(mixed * coef_t[sub, q].astype(f32))
            back = dot3(tab_high[q], tab_low[q], high, low)
            for s in range(SLOTS):
                real = back[s * COLS:(s + 1) * COLS]
                imag = back[SIZE + s * COLS:SIZE + (s + 1) * COLS]
                last = real[:, 128:] + pltpu.roll(imag[:, 128:], 64, 1)
                values = jnp.concatenate([real[:, :128], imag[:, :128], last], axis=1)
                spread(values, q * SLOTS + s, COLS)
                top = jnp.maximum(top, peak(values))
            return top

        encode(lax.fori_loop(0, SLOTS, latitude, jnp.zeros((1, 128), f32)), 2 + sub)
        start(2 + sub)

    def spectral(sub, step):
        arrive(2 + sub)
        sent(sub)
        last = step == STEPS - 1

        def operands(s, carry):
            for q in range(SLOTS):
                values = jnp.concatenate([gathered(q * SLOTS + s, part) for part in range(PARTS)], axis=1)
                high, low = split(values)
                rows = slice(q * COLS, (q + 1) * COLS)
                for half, value in ((op_high, high), (op_low, low)):
                    half[s, rows, :] = value[:, :SIZE]
                    half[s, SIZE + q * COLS:SIZE + (q + 1) * COLS, :128] = value[:, SIZE:]
            return carry

        lax.fori_loop(0, SLOTS, operands, 0)

        def slot(s, top):
            cut = slice(SIZE, 2 * SIZE)
            inc = jnp.concatenate([
                dot3(inv_high[s], inv_low[s], op_high[s, :SIZE], op_low[s, :SIZE]),
                dot3(inv_high[s], inv_low[s], op_high[s, cut, :128], op_low[s, cut, :128]),
            ], axis=1)
            if step == 0:
                before = jnp.transpose(in_order(forcing[sub, s]))
            else:
                before = state[sub, s]
            after = damp[...] * before + inc
            if not last:
                state[sub, s] = after
                high, low = split(after)
                four = dot3(fwd_high[s], fwd_low[s], high, low)
                for q in range(SLOTS):
                    spread(four[q * COLS:(q + 1) * COLS], q * SLOTS + s, COLS)
                return jnp.maximum(top, peak(four))
            state[sub, s] = after
            return jnp.maximum(top, peak(after))

        top = lax.fori_loop(0, SLOTS, slot, jnp.zeros((1, 128), f32))
        if not last:
            encode(top, sub)
            start(sub)
        else:
            sent(2 + sub)

            @pl.when(sub == 0)
            def _():
                for s in range(SLOTS):
                    for part in range(PARTS):
                        stage[part, s * SIZE:(s + 1) * SIZE, :] = state[0, s, :, part * 128:(part + 1) * 128]
                encode(top, 0)
                pltpu.make_async_remote_copy(
                    src_ref=send_scale.at[0], dst_ref=passed_scale,
                    send_sem=pass_sem.at[0], recv_sem=pass_sem.at[1],
                    device_id=(win - 1, col), device_id_type=MESH,
                ).start()
                pltpu.make_async_remote_copy(
                    src_ref=send.at[0], dst_ref=passed,
                    send_sem=pass_sem.at[2], recv_sem=pass_sem.at[3],
                    device_id=(win - 1, col), device_id_type=MESH,
                ).start()

    for step in range(STEPS):
        for phase in (grid, spectral):
            def both(sub, carry):
                @pl.when(live(sub))
                def _():
                    phase(sub, step)

                return carry

            lax.fori_loop(0, 2, both, 0)

    def write(index, s, result):
        flat = jnp.transpose(result)
        for r in range(2):
            out[index, s, r, :128] = forcing[index, s, r, :128] - flat[r * 128:(r + 1) * 128]
            out[index, s, r, 128:] = forcing[index, s, r, 128:] - flat[256 + r * 64:256 + (r + 1) * 64]

    def near_result(s, carry):
        write(0, s, state[1, s])
        return carry

    lax.fori_loop(0, SLOTS, near_result, 0)

    @pl.when(win > 0)
    def _():
        pltpu.make_async_copy(send_scale.at[0], send_scale.at[0], pass_sem.at[0]).wait()
        pltpu.make_async_copy(send.at[0], send.at[0], pass_sem.at[2]).wait()

    @pl.when(win < 3)
    def _():
        pltpu.make_async_copy(passed_scale, passed_scale, pass_sem.at[1]).wait()
        pltpu.make_async_copy(passed, passed, pass_sem.at[3]).wait()
        decode(
            lambda d, part: passed[d, :, part * 128:(part + 1) * 128],
            lambda d: passed_scale[...],
        )

        def far_result(s, carry):
            rows = pl.ds(pl.multiple_of(s * SIZE, SIZE), SIZE)
            write(1, s, jnp.concatenate([stage[part, rows, :] for part in range(PARTS)], axis=1))
            return carry

        lax.fori_loop(0, SLOTS, far_result, 0)

    @pl.when(win == 3)
    def _():
        def own(s, carry):
            out[1, s] = forcing[1, s]
            return carry

        lax.fori_loop(0, SLOTS, own, 0)


def shards(forcing, coefficients, legendre, weights, damping, mixing, points, wavenumbers):
    vmem = pl.BlockSpec(memory_space=pltpu.VMEM)
    smem = pl.BlockSpec(memory_space=pltpu.SMEM)
    dma = pltpu.SemaphoreType.DMA
    return pl.pallas_call(
        kernel,
        out_shape=jax.ShapeDtypeStruct(forcing.shape, f32),
        in_specs=[vmem] * 7 + [smem] * 2,
        out_specs=vmem,
        scratch_shapes=[
            pltpu.VMEM((4, COLS, ROWS, LANES), jnp.int16),
            pltpu.VMEM((4, COLS, ROWS, LANES), jnp.int16),
            pltpu.VMEM((4, 1, 128), f32),
            pltpu.VMEM((4, COLS, 1, 128), f32),
            pltpu.VMEM((COLS, ROWS, LANES), jnp.int16),
            pltpu.VMEM((1, 128), f32),
            pltpu.VMEM((PARTS, COLS * ROWS, 128), f32),
            pltpu.VMEM((2, SLOTS, SIZE, LANES), f32),
            pltpu.VMEM((SLOTS, SIZE, SIZE), bf16),
            pltpu.VMEM((SLOTS, SIZE, SIZE), bf16),
            pltpu.VMEM((SLOTS, SIZE, SIZE), bf16),
            pltpu.VMEM((SLOTS, SIZE, SIZE), bf16),
            pltpu.VMEM((SIZE, LANES), f32),
            pltpu.VMEM((SIZE, SIZE), f32),
            pltpu.VMEM((SIZE, SIZE), bf16),
            pltpu.VMEM((SIZE, SIZE), bf16),
            pltpu.VMEM((SIZE, SIZE), bf16),
            pltpu.VMEM((SIZE, SIZE), bf16),
            pltpu.VMEM((SLOTS, WIDTH, WIDTH), bf16),
            pltpu.VMEM((SLOTS, WIDTH, WIDTH), bf16),
            pltpu.VMEM((SLOTS, WIDTH, WIDTH), bf16),
            pltpu.VMEM((SLOTS, WIDTH, WIDTH), bf16),
            pltpu.VMEM((2, SLOTS, WIDTH, SIZE), bf16),
            pltpu.VMEM((SLOTS, WIDTH, SIZE), bf16),
            pltpu.VMEM((SLOTS, WIDTH, SIZE), bf16),
            dma((4,)), dma((4,)), dma((4,)), dma((4,)), dma((4,)),
        ],
        compiler_params=pltpu.CompilerParams(
            collective_id=0, has_side_effects=True, vmem_limit_bytes=56 * 2**20
        ),
        name="adjoint",
    )(
        forcing, coefficients, legendre, weights.reshape(1, SIZE), damping, mixing,
        wavenumbers.reshape(1, SIZE), points, wavenumbers,
    )


def solution(mesh):
    in_specs = (
        P("win", "col", None, None, None),
        P("win", "col", None, None),
        P("col", None, None),
        P(),
        P(),
        P(),
        P(),
        P(),
    )
    out_specs = P("win", "col", None, None, None)
    return jax.shard_map(shards, mesh=mesh, in_specs=in_specs, out_specs=out_specs, check_vma=False)
```

```python
import functools
import math

import jax
import jax.numpy as jnp
from jax import lax
from jax.experimental import pallas as pl
from jax.experimental.pallas import tpu as pltpu
from jax.sharding import PartitionSpec as P

STEPS = 2
SLOTS = 4
COLS = 64
ROWS = 16
LEVELS = 192
SIZE = 256
WIDTH = 512
LANES = 384
PARTS = 3
RELAYED = 8
GROUP = 8
TOP = 32767.0

f32 = jnp.float32
bf16 = jnp.bfloat16
MESH = pl.DeviceIdType.MESH


def split(values):
    high = values.astype(bf16)
    return high, (values - high.astype(f32)).astype(bf16)


def dot(a, b):
    return lax.dot_general(a, b, (((1,), (0,)), ((), ())), preferred_element_type=f32)


def dot_t(a, b):
    return lax.dot_general(a, b, (((1,), (1,)), ((), ())), preferred_element_type=f32)


def dot3(a_high, a_low, b_high, b_low, product=dot):
    return product(a_high, b_high) + (product(a_high, b_low) + product(a_low, b_high))


def widened(row):
    return jnp.concatenate([row] * PARTS, axis=1)


def kernel(
    forcing, coefs, legendre, weights, damping, mixing, row_numbers, points, numbers,
    out,
    send, recv, send_scale, recv_scale, relay, passed, passed_scale,
    stage, state, fwd_high, fwd_low, inv_high, inv_low, damp, mix_pad, mix_high, mix_low,
    perm, eye, tab_high, tab_low, tabt_high, tabt_low, coef_t, op_high, op_low,
    send_sem, recv_sem, relay_sem, forward_sem,
    near_send_sem, near_recv_sem, far_send_sem, far_recv_sem, pass_sem,
):
    win = lax.axis_index("win")
    col = lax.axis_index("col")
    at_z, at_y, at_x = col // 16, (col // 4) % 4, col % 4
    group, member = col // GROUP, col % GROUP
    lighter = jnp.where(win < 2, 3, 1)

    def partner(k):
        z = (at_z + k // 16) % 4
        y = (at_y + (k // 4) % 4) % 4
        x = (at_x + k % 4) % 4
        return z * 16 + y * 4 + x

    barrier = pltpu.get_barrier_semaphore()

    def greet(k, carry):
        pl.semaphore_signal(barrier, inc=1, device_id=(win, partner(k)), device_id_type=MESH)
        return carry

    lax.fori_loop(1, COLS, greet, 0)

    @pl.when(win > 0)
    def _():
        pl.semaphore_signal(barrier, inc=1, device_id=(win - 1, col), device_id_type=MESH)

    @pl.when(win < 3)
    def _():
        pl.semaphore_signal(barrier, inc=1, device_id=(win + 1, col), device_id_type=MESH)

    def in_order(x):
        return jnp.concatenate([x[0, :128], x[1, :128], x[0, 128:], x[1, 128:]], axis=0)

    def spread(values, row, rows):
        for part in range(PARTS):
            stage[part, pl.ds(row, rows, stride=ROWS), :] = values[:, part * 128:(part + 1) * 128]

    def gathered(row, part):
        return stage[part, pl.ds(row, COLS, stride=ROWS), :]

    def peak(values):
        top = jnp.max(jnp.abs(values), axis=0, keepdims=True)
        return jnp.maximum(jnp.maximum(top[:, :128], top[:, 128:256]), top[:, 256:384])

    def encode(top, buf):
        top = jnp.maximum(top, 1e-30)
        send_scale[buf] = top * (1.0 / TOP)
        inverse = TOP / top

        def one(d, carry):
            for part in range(PARTS):
                code = jnp.round(stage[part, pl.ds(pl.multiple_of(d * ROWS, ROWS), ROWS), :] * inverse)
                send[buf, d, :, part * 128:(part + 1) * 128] = code.astype(jnp.int32).astype(jnp.int16)
            return carry

        lax.fori_loop(0, COLS, one, 0, unroll=4)

    def decode(codes, scales):
        def one(d, carry):
            scale = scales(d)
            for part in range(PARTS):
                code = codes(d, part).astype(jnp.int32).astype(f32)
                stage[part, pl.ds(pl.multiple_of(d * ROWS, ROWS), ROWS), :] = code * scale
            return carry

        lax.fori_loop(0, COLS, one, 0, unroll=4)

    def copy_to(target, src, dst, send_by, recv_by):
        pltpu.make_async_remote_copy(
            src_ref=src, dst_ref=dst, send_sem=send_by, recv_sem=recv_by,
            device_id=(win, target), device_id_type=MESH,
        ).start()

    def wait_blocks(count, sem):
        some = recv.at[0, pl.ds(0, count)]
        pltpu.make_async_copy(some, some, sem).wait()

    def wait_scales(count, sem):
        some = recv_scale.at[0, pl.ds(0, count)]
        pltpu.make_async_copy(some, some, sem).wait()

    def start(buf):
        def block(target):
            copy_to(target, send.at[buf, target], recv.at[buf, col], send_sem.at[buf], recv_sem.at[buf])

        def scale(k, carry):
            target = group * GROUP + (member + k) % GROUP
            copy_to(target, send_scale.at[buf], recv_scale.at[buf, col], near_send_sem.at[buf], near_recv_sem.at[buf])
            return carry

        def opposite(k, carry):
            block(((at_z + 2) % 4) * 16 + (2 + (at_y + k // 4) % 2) * 4 + (at_x + k) % 4)
            return carry

        def beside(k, carry):
            place = ((at_y + k // 4) % 4) * 4 + (at_x + k) % 4
            block(((at_z + 1) % 4) * 16 + place)
            block(((at_z + 3) % 4) * 16 + place)
            return carry

        def level(k, carry):
            block(at_z * 16 + ((at_y + k // 4) % 4) * 4 + (at_x + k) % 4)
            return carry

        recv_scale[buf, col] = send_scale[buf]
        lax.fori_loop(1, GROUP, scale, 0)
        copy_to(
            ((at_z + lighter) % 4) * 16 + at_y * 4 + at_x,
            send.at[buf, pl.ds(((at_z + 2) % 4) * 16, RELAYED)], relay.at[buf], send_sem.at[buf], relay_sem.at[buf],
        )
        lax.fori_loop(0, RELAYED, opposite, 0)
        lax.fori_loop(0, 16, beside, 0)
        lax.fori_loop(1, 16, level, 0)
        recv[buf, col] = send[buf, col]

    def forward(buf):
        wait_blocks(RELAYED, relay_sem.at[buf])
        source = ((at_z + 4 - lighter) % 4) * 16 + at_y * 4 + at_x

        def block(k, carry):
            place = ((at_y + k // 4) % 2) * 4 + (at_x + k) % 4
            copy_to(
                ((at_z + lighter) % 4) * 16 + place,
                relay.at[buf, place], recv.at[buf, source], forward_sem.at[buf], recv_sem.at[buf],
            )
            return carry

        lax.fori_loop(0, RELAYED, block, 0)
        wait_scales(GROUP - 1, near_recv_sem.at[buf])

        def scales(k, carry):
            some = recv_scale.at[buf, pl.ds(group * GROUP, GROUP)]
            copy_to(((group + k) % GROUP) * GROUP + member, some, some, far_send_sem.at[buf], far_recv_sem.at[buf])
            return carry

        lax.fori_loop(1, GROUP, scales, 0)

    def settle(buf):
        wait_blocks(RELAYED, forward_sem.at[buf])
        wait_scales((GROUP - 1) * GROUP, far_send_sem.at[buf])

    def sent(buf):
        wait_blocks(COLS - 1, send_sem.at[buf])
        wait_scales(GROUP - 1, near_send_sem.at[buf])

    def arrive(buf, other, more=True):
        wait_blocks(COLS - 1, recv_sem.at[buf])
        wait_scales((GROUP - 1) * GROUP, far_recv_sem.at[buf])

        @pl.when(jnp.logical_and(win > 0, more))
        def _():
            forward(other)

        decode(
            lambda d, part: recv[buf, d, :, part * 128:(part + 1) * 128],
            lambda d: recv_scale[buf, d],
        )

    def follow(sub, buf):
        @pl.when(win == 0)
        def _():
            forward(buf)

    def live(sub):
        return jnp.logical_or(sub > 0, win > 0)

    row = lax.broadcasted_iota(jnp.int32, (SIZE, SIZE), 0)
    lane = lax.broadcasted_iota(jnp.int32, (SIZE, SIZE), 1)
    perm[...] = (row == 4 * (lane % COLS) + lane // COLS).astype(f32).astype(bf16)
    eye[...] = (row == lane).astype(f32).astype(bf16)
    permt = (lane == 4 * (row % COLS) + row // COLS).astype(f32).astype(bf16)

    def masked(s):
        keep = (row >= numbers[col * SLOTS + s]).astype(f32)
        return legendre[s] * keep

    def forward_table(s, carry):
        high, low = split(masked(s))
        fwd_high[s] = dot_t(permt, high).astype(bf16)
        fwd_low[s] = dot_t(permt, low).astype(bf16)
        return carry

    lax.fori_loop(0, SLOTS, forward_table, 0)

    def first(sub, carry):
        @pl.when(live(sub))
        def _():
            def slot(s, top):
                high, low = split(in_order(forcing[sub, s]))
                four = dot3(fwd_high[s], fwd_low[s], high, low, dot_t)
                for q in range(SLOTS):
                    spread(four[q * COLS:(q + 1) * COLS], q * SLOTS + s, COLS)
                return jnp.maximum(top, peak(four))

            encode(lax.fori_loop(0, SLOTS, slot, jnp.zeros((1, 128), f32)), sub)

            @pl.when(sub == jnp.where(win > 0, 0, 1))
            def _():
                pl.semaphore_wait(barrier, COLS - 1 + jnp.where(win > 0, 1, 0) + jnp.where(win < 3, 1, 0))

            @pl.when(jnp.logical_and(win > 0, sub == 1))
            def _():
                forward(0)

            start(sub)
            follow(sub, sub)

        return carry

    lax.fori_loop(0, 2, first, 0)

    def inverse_table(s, carry):
        high, low = split(masked(s) * weights[...])
        inv_high[s] = dot(high, perm[...]).astype(bf16)
        inv_low[s] = dot(low, perm[...]).astype(bf16)
        return carry

    lax.fori_loop(0, SLOTS, inverse_table, 0)

    mix_pad[...] = jnp.zeros((SIZE, SIZE), f32)
    mix_pad[:LEVELS, :LEVELS] = mixing[...]
    high, low = split(mix_pad[...])
    mix_high[...] = high
    mix_low[...] = low

    damp_t = jnp.transpose(jnp.concatenate([damping[...], damping[128:]], axis=0))
    damp[...] = jnp.concatenate([damp_t[:, :128], damp_t[:, :128], damp_t[:, 128:]], axis=1)

    wave = jnp.broadcast_to(row_numbers[...].astype(f32).astype(bf16), (16, SIZE))
    wave = dot(wave, perm[...])[:1]

    def table(q, carry):
        count = points[col * SLOTS + q]
        count_f = jnp.full((1, SIZE), count, jnp.int32).astype(f32)
        part_of = 1.0 / count_f

        def angles(rows, step):
            j = (step * lax.broadcasted_iota(jnp.int32, (rows, SIZE), 0)).astype(f32)
            product = j * wave
            rest = product - jnp.floor(product * part_of) * count_f
            rest = jnp.where(rest < 0.0, rest + count_f, rest)
            rest = jnp.where(rest >= count_f, rest - count_f, rest)
            angle = (2.0 * math.pi) * rest / count_f
            return jnp.cos(angle), jnp.sin(angle)

        cos_a, sin_a = angles(WIDTH // 16, 16)
        cos_b, sin_b = angles(16, 1)
        near = lax.broadcasted_iota(jnp.int32, (16, SIZE), 0)
        for a in range(WIDTH // 16):
            keep = (near + 16 * a < count).astype(f32)
            ca, sa = cos_a[a:a + 1] , sin_a[a:a + 1]
            cos = (ca * cos_b - sa * sin_b) * keep
            sin = (sa * cos_b + ca * sin_b) * keep
            for r, value in ((0, cos), (1, -sin)):
                high, low = split(value)
                tabt_high[q, a * 16:(a + 1) * 16, r * SIZE:(r + 1) * SIZE] = high
                tabt_low[q, a * 16:(a + 1) * 16, r * SIZE:(r + 1) * SIZE] = low
        for r in range(2):
            cut = slice(r * SIZE, (r + 1) * SIZE)
            tab_high[q, cut, :] = dot_t(eye[...], tabt_high[q, :, cut]).astype(bf16)
            tab_low[q, cut, :] = dot_t(eye[...], tabt_low[q, :, cut]).astype(bf16)
        for sub in range(2):
            padded = jnp.concatenate([coefs[sub, q], jnp.zeros((SIZE - LEVELS, WIDTH), bf16)], axis=0)
            for h in range(2):
                cut = slice(h * SIZE, (h + 1) * SIZE)
                coef_t[sub, q, cut, :] = dot_t(eye[...], padded[:, cut]).astype(bf16)
        return carry

    lax.fori_loop(0, SLOTS, table, 0)

    def grid(sub, step):
        arrive(sub, jnp.where(sub == 0, 1, 2))
        if step > 0:
            sent(2 + sub)

        def latitude(q, carry):
            for s in range(SLOTS):
                at = q * SLOTS + s
                last = gathered(at, 2)
                real = jnp.concatenate([gathered(at, 0), last], axis=1)
                imag = jnp.concatenate([gathered(at, 1), pltpu.roll(last, 64, 1)], axis=1)
                for r, value in ((0, real), (1, imag)):
                    high, low = split(value)
                    rows = slice(r * SIZE + s * COLS, r * SIZE + (s + 1) * COLS)
                    op_high[q, rows, :] = high
                    op_low[q, rows, :] = low
            return carry

        lax.fori_loop(0, SLOTS, latitude, 0)

        def latitude(q, top):
            values = dot3(tabt_high[q], tabt_low[q], op_high[q], op_low[q])
            high, low = split(values)
            mixed = dot3(high, low, mix_high[...], mix_low[...])
            high, low = split(mixed * coef_t[sub, q].astype(f32))
            back = dot3(tab_high[q], tab_low[q], high, low)
            for s in range(SLOTS):
                real = back[s * COLS:(s + 1) * COLS]
                imag = back[SIZE + s * COLS:SIZE + (s + 1) * COLS]
                last = real[:, 128:] + pltpu.roll(imag[:, 128:], 64, 1)
                values = jnp.concatenate([real[:, :128], imag[:, :128], last], axis=1)
                spread(values, q * SLOTS + s, COLS)
                top = jnp.maximum(top, peak(values))
            return top

        encode(lax.fori_loop(0, SLOTS, latitude, jnp.zeros((1, 128), f32)), 2 + sub)
        settle(sub)
        start(2 + sub)
        follow(sub, 2 + sub)

    def spectral(sub, step):
        last = step == STEPS - 1
        arrive(2 + sub, jnp.where(sub == 0, 3, 0), jnp.logical_or(not last, sub == 0))
        sent(sub)

        def operands(s, carry):
            for q in range(SLOTS):
                values = jnp.concatenate([gathered(q * SLOTS + s, part) for part in range(PARTS)], axis=1)
                high, low = split(values)
                rows = slice(q * COLS, (q + 1) * COLS)
                for half, value in ((op_high, high), (op_low, low)):
                    half[s, rows, :] = value[:, :SIZE]
                    half[s, SIZE + q * COLS:SIZE + (q + 1) * COLS, :128] = value[:, SIZE:]
            return carry

        lax.fori_loop(0, SLOTS, operands, 0)

        def slot(s, top):
            cut = slice(SIZE, 2 * SIZE)
            inc = jnp.concatenate([
                dot3(inv_high[s], inv_low[s], op_high[s, :SIZE], op_low[s, :SIZE]),
                dot3(inv_high[s], inv_low[s], op_high[s, cut, :128], op_low[s, cut, :128]),
            ], axis=1)
            if step == 0:
                before = jnp.transpose(in_order(forcing[sub, s]))
            else:
                before = state[sub, s]
            after = damp[...] * before + inc
            if not last:
                state[sub, s] = after
                high, low = split(after)
                four = dot3(fwd_high[s], fwd_low[s], high, low)
                for q in range(SLOTS):
                    spread(four[q * COLS:(q + 1) * COLS], q * SLOTS + s, COLS)
                return jnp.maximum(top, peak(four))
            state[sub, s] = after
            return jnp.maximum(top, peak(after))

        top = lax.fori_loop(0, SLOTS, slot, jnp.zeros((1, 128), f32))
        if not last:
            encode(top, sub)
            settle(2 + sub)
            start(sub)
            follow(sub, sub)
        else:
            sent(2 + sub)
            settle(2 + sub)

            @pl.when(sub == 0)
            def _():
                for s in range(SLOTS):
                    for part in range(PARTS):
                        stage[part, s * SIZE:(s + 1) * SIZE, :] = state[0, s, :, part * 128:(part + 1) * 128]
                encode(top, 0)
                pltpu.make_async_remote_copy(
                    src_ref=send_scale.at[0], dst_ref=passed_scale,
                    send_sem=pass_sem.at[0], recv_sem=pass_sem.at[1],
                    device_id=(win - 1, col), device_id_type=MESH,
                ).start()
                pltpu.make_async_remote_copy(
                    src_ref=send.at[0], dst_ref=passed,
                    send_sem=pass_sem.at[2], recv_sem=pass_sem.at[3],
                    device_id=(win - 1, col), device_id_type=MESH,
                ).start()

    for step in range(STEPS):
        for phase in (grid, spectral):
            def both(sub, carry):
                @pl.when(live(sub))
                def _():
                    phase(sub, step)

                return carry

            lax.fori_loop(0, 2, both, 0)

    def write(index, s, result):
        flat = jnp.transpose(result)
        for r in range(2):
            out[index, s, r, :128] = forcing[index, s, r, :128] - flat[r * 128:(r + 1) * 128]
            out[index, s, r, 128:] = forcing[index, s, r, 128:] - flat[256 + r * 64:256 + (r + 1) * 64]

    def near_result(s, carry):
        write(0, s, state[1, s])
        return carry

    lax.fori_loop(0, SLOTS, near_result, 0)

    @pl.when(win > 0)
    def _():
        pltpu.make_async_copy(send_scale.at[0], send_scale.at[0], pass_sem.at[0]).wait()
        pltpu.make_async_copy(send.at[0], send.at[0], pass_sem.at[2]).wait()

    @pl.when(win < 3)
    def _():
        pltpu.make_async_copy(passed_scale, passed_scale, pass_sem.at[1]).wait()
        pltpu.make_async_copy(passed, passed, pass_sem.at[3]).wait()
        decode(
            lambda d, part: passed[d, :, part * 128:(part + 1) * 128],
            lambda d: passed_scale[...],
        )

        def far_result(s, carry):
            rows = pl.ds(pl.multiple_of(s * SIZE, SIZE), SIZE)
            write(1, s, jnp.concatenate([stage[part, rows, :] for part in range(PARTS)], axis=1))
            return carry

        lax.fori_loop(0, SLOTS, far_result, 0)

    @pl.when(win == 3)
    def _():
        def own(s, carry):
            out[1, s] = forcing[1, s]
            return carry

        lax.fori_loop(0, SLOTS, own, 0)


def shards(forcing, coefficients, legendre, weights, damping, mixing, points, wavenumbers):
    vmem = pl.BlockSpec(memory_space=pltpu.VMEM)
    smem = pl.BlockSpec(memory_space=pltpu.SMEM)
    dma = pltpu.SemaphoreType.DMA
    return pl.pallas_call(
        kernel,
        out_shape=jax.ShapeDtypeStruct(forcing.shape, f32),
        in_specs=[vmem] * 7 + [smem] * 2,
        out_specs=vmem,
        scratch_shapes=[
            pltpu.VMEM((4, COLS, ROWS, LANES), jnp.int16),
            pltpu.VMEM((4, COLS, ROWS, LANES), jnp.int16),
            pltpu.VMEM((4, 1, 128), f32),
            pltpu.VMEM((4, COLS, 1, 128), f32),
            pltpu.VMEM((4, RELAYED, ROWS, LANES), jnp.int16),
            pltpu.VMEM((COLS, ROWS, LANES), jnp.int16),
            pltpu.VMEM((1, 128), f32),
            pltpu.VMEM((PARTS, COLS * ROWS, 128), f32),
            pltpu.VMEM((2, SLOTS, SIZE, LANES), f32),
            pltpu.VMEM((SLOTS, SIZE, SIZE), bf16),
            pltpu.VMEM((SLOTS, SIZE, SIZE), bf16),
            pltpu.VMEM((SLOTS, SIZE, SIZE), bf16),
            pltpu.VMEM((SLOTS, SIZE, SIZE), bf16),
            pltpu.VMEM((SIZE, LANES), f32),
            pltpu.VMEM((SIZE, SIZE), f32),
            pltpu.VMEM((SIZE, SIZE), bf16),
            pltpu.VMEM((SIZE, SIZE), bf16),
            pltpu.VMEM((SIZE, SIZE), bf16),
            pltpu.VMEM((SIZE, SIZE), bf16),
            pltpu.VMEM((SLOTS, WIDTH, WIDTH), bf16),
            pltpu.VMEM((SLOTS, WIDTH, WIDTH), bf16),
            pltpu.VMEM((SLOTS, WIDTH, WIDTH), bf16),
            pltpu.VMEM((SLOTS, WIDTH, WIDTH), bf16),
            pltpu.VMEM((2, SLOTS, WIDTH, SIZE), bf16),
            pltpu.VMEM((SLOTS, WIDTH, SIZE), bf16),
            pltpu.VMEM((SLOTS, WIDTH, SIZE), bf16),
            dma((4,)), dma((4,)), dma((4,)), dma((4,)),
            dma((4,)), dma((4,)), dma((4,)), dma((4,)), dma((4,)),
        ],
        compiler_params=pltpu.CompilerParams(
            collective_id=0, has_side_effects=True, vmem_limit_bytes=56 * 2**20
        ),
        name="adjoint",
    )(
        forcing, coefficients, legendre, weights.reshape(1, SIZE), damping, mixing,
        wavenumbers.reshape(1, SIZE), points, wavenumbers,
    )


def solution(mesh):
    in_specs = (
        P("win", "col", None, None, None),
        P("win", "col", None, None),
        P("col", None, None),
        P(),
        P(),
        P(),
        P(),
        P(),
    )
    out_specs = P("win", "col", None, None, None)
    return jax.shard_map(shards, mesh=mesh, in_specs=in_specs, out_specs=out_specs, check_vma=False)
```

```python
import functools
import math

import jax
import jax.numpy as jnp
from jax import lax
from jax.experimental import pallas as pl
from jax.experimental.pallas import tpu as pltpu
from jax.sharding import PartitionSpec as P

STEPS = 2
SLOTS = 4
COLS = 64
ROWS = 16
LEVELS = 192
SIZE = 256
WIDTH = 512
LANES = 384
PARTS = 3
RELAYED = 8
GROUP = 8
UNROLL = 4
TOP = 32767.0

f32 = jnp.float32
bf16 = jnp.bfloat16
MESH = pl.DeviceIdType.MESH


def split(values):
    high = values.astype(bf16)
    return high, (values - high.astype(f32)).astype(bf16)


def dot(a, b):
    return lax.dot_general(a, b, (((1,), (0,)), ((), ())), preferred_element_type=f32)


def dot_t(a, b):
    return lax.dot_general(a, b, (((1,), (1,)), ((), ())), preferred_element_type=f32)


def dot3(a_high, a_low, b_high, b_low, product=dot):
    return product(a_high, b_high) + (product(a_high, b_low) + product(a_low, b_high))


def kernel(
    forcing_in, coefs_in, legendre_in, weights, damping, mixing, row_numbers, points, numbers,
    out_in,
    forcing, coefs, legendre, out,
    send, recv, send_scale, recv_scale, relay, passed, passed_scale,
    stage, state, fwd_high, fwd_low, inv_high, inv_low, damp, mix_pad, mix_high, mix_low,
    perm, eye, tab_high, tab_low, tabt_high, tabt_low, coef_t, op_high, op_low,
    send_sem, recv_sem, relay_sem, forward_sem,
    near_send_sem, near_recv_sem, far_send_sem, far_recv_sem, pass_sem, load_sem, store_sem,
):
    win = lax.axis_index("win")
    col = lax.axis_index("col")
    at_z, at_y, at_x = col // 16, (col // 4) % 4, col % 4
    group, member = col // GROUP, col % GROUP
    lighter = jnp.where(win < 2, 3, 1)

    def partner(k):
        z = (at_z + k // 16) % 4
        y = (at_y + (k // 4) % 4) % 4
        x = (at_x + k % 4) % 4
        return z * 16 + y * 4 + x

    loads = [
        pltpu.make_async_copy(legendre_in, legendre, load_sem.at[2]),
        pltpu.make_async_copy(forcing_in.at[0], forcing.at[0], load_sem.at[0]),
        pltpu.make_async_copy(forcing_in.at[1], forcing.at[1], load_sem.at[1]),
        pltpu.make_async_copy(coefs_in, coefs, load_sem.at[3]),
    ]
    for load in loads:
        load.start()

    barrier = pltpu.get_barrier_semaphore()

    def greet(k, carry):
        pl.semaphore_signal(barrier, inc=1, device_id=(win, partner(k)), device_id_type=MESH)
        return carry

    lax.fori_loop(1, COLS, greet, 0)

    @pl.when(win > 0)
    def _():
        pl.semaphore_signal(barrier, inc=1, device_id=(win - 1, col), device_id_type=MESH)

    @pl.when(win < 3)
    def _():
        pl.semaphore_signal(barrier, inc=1, device_id=(win + 1, col), device_id_type=MESH)

    def in_order(x):
        return jnp.concatenate([x[0, :128], x[1, :128], x[0, 128:], x[1, 128:]], axis=0)

    def spread(values, row, rows):
        for part in range(PARTS):
            stage[part, pl.ds(row, rows, stride=ROWS), :] = values[:, part * 128:(part + 1) * 128]

    def gathered(row, part):
        return stage[part, pl.ds(row, COLS, stride=ROWS), :]

    def peak(values):
        top = jnp.max(jnp.abs(values), axis=0, keepdims=True)
        return jnp.maximum(jnp.maximum(top[:, :128], top[:, 128:256]), top[:, 256:384])

    def encode(top, buf):
        top = jnp.maximum(top, 1e-30)
        send_scale[buf] = top * (1.0 / TOP)
        inverse = TOP / top

        def one(d, carry):
            for part in range(PARTS):
                code = jnp.round(stage[part, pl.ds(pl.multiple_of(d * ROWS, ROWS), ROWS), :] * inverse)
                send[buf, d, :, part * 128:(part + 1) * 128] = code.astype(jnp.int32).astype(jnp.int16)
            return carry

        lax.fori_loop(0, COLS, one, 0, unroll=4)

    def decode(codes, scales):
        def one(d, carry):
            scale = scales(d)
            for part in range(PARTS):
                code = codes(d, part).astype(jnp.int32).astype(f32)
                stage[part, pl.ds(pl.multiple_of(d * ROWS, ROWS), ROWS), :] = code * scale
            return carry

        lax.fori_loop(0, COLS, one, 0, unroll=4)

    def copy_to(target, src, dst, send_by, recv_by):
        pltpu.make_async_remote_copy(
            src_ref=src, dst_ref=dst, send_sem=send_by, recv_sem=recv_by,
            device_id=(win, target), device_id_type=MESH,
        ).start()

    def wait_blocks(count, sem):
        some = recv.at[0, pl.ds(0, count)]
        pltpu.make_async_copy(some, some, sem).wait()

    def wait_scales(count, sem):
        some = recv_scale.at[0, pl.ds(0, count)]
        pltpu.make_async_copy(some, some, sem).wait()

    def start(buf):
        def block(target):
            copy_to(target, send.at[buf, target], recv.at[buf, col], send_sem.at[buf], recv_sem.at[buf])

        def scale(k, carry):
            target = group * GROUP + (member + k) % GROUP
            copy_to(target, send_scale.at[buf], recv_scale.at[buf, col], near_send_sem.at[buf], near_recv_sem.at[buf])
            return carry

        def opposite(k, carry):
            block(((at_z + 2) % 4) * 16 + (2 + (at_y + k // 4) % 2) * 4 + (at_x + k) % 4)
            return carry

        def beside(k, carry):
            place = ((at_y + k // 4) % 4) * 4 + (at_x + k) % 4
            block(((at_z + 1) % 4) * 16 + place)
            block(((at_z + 3) % 4) * 16 + place)
            return carry

        def level(k, carry):
            block(at_z * 16 + ((at_y + k // 4) % 4) * 4 + (at_x + k) % 4)
            return carry

        recv_scale[buf, col] = send_scale[buf]
        lax.fori_loop(1, GROUP, scale, 0)
        copy_to(
            ((at_z + lighter) % 4) * 16 + at_y * 4 + at_x,
            send.at[buf, pl.ds(((at_z + 2) % 4) * 16, RELAYED)], relay.at[buf], send_sem.at[buf], relay_sem.at[buf],
        )
        lax.fori_loop(0, RELAYED, opposite, 0)
        lax.fori_loop(0, 16, beside, 0)
        lax.fori_loop(1, 16, level, 0)
        recv[buf, col] = send[buf, col]

    def forward(buf):
        wait_blocks(RELAYED, relay_sem.at[buf])
        source = ((at_z + 4 - lighter) % 4) * 16 + at_y * 4 + at_x

        def block(k, carry):
            place = ((at_y + k // 4) % 2) * 4 + (at_x + k) % 4
            copy_to(
                ((at_z + lighter) % 4) * 16 + place,
                relay.at[buf, place], recv.at[buf, source], forward_sem.at[buf], recv_sem.at[buf],
            )
            return carry

        lax.fori_loop(0, RELAYED, block, 0)
        wait_scales(GROUP - 1, near_recv_sem.at[buf])

        def scales(k, carry):
            some = recv_scale.at[buf, pl.ds(group * GROUP, GROUP)]
            copy_to(((group + k) % GROUP) * GROUP + member, some, some, far_send_sem.at[buf], far_recv_sem.at[buf])
            return carry

        lax.fori_loop(1, GROUP, scales, 0)

    def settle(buf):
        wait_blocks(RELAYED, forward_sem.at[buf])
        wait_scales((GROUP - 1) * GROUP, far_send_sem.at[buf])

    def sent(buf):
        wait_blocks(COLS - 1, send_sem.at[buf])
        wait_scales(GROUP - 1, near_send_sem.at[buf])

    def arrive(buf, other, more=True):
        wait_blocks(COLS - 1, recv_sem.at[buf])
        wait_scales((GROUP - 1) * GROUP, far_recv_sem.at[buf])

        @pl.when(jnp.logical_and(win > 0, more))
        def _():
            forward(other)

        decode(
            lambda d, part: recv[buf, d, :, part * 128:(part + 1) * 128],
            lambda d: recv_scale[buf, d],
        )

    def follow(sub, buf):
        @pl.when(win == 0)
        def _():
            forward(buf)

    def live(sub):
        return jnp.logical_or(sub > 0, win > 0)

    row = lax.broadcasted_iota(jnp.int32, (SIZE, SIZE), 0)
    lane = lax.broadcasted_iota(jnp.int32, (SIZE, SIZE), 1)
    perm[...] = (row == 4 * (lane % COLS) + lane // COLS).astype(f32).astype(bf16)
    eye[...] = (row == lane).astype(f32).astype(bf16)
    permt = (lane == 4 * (row % COLS) + row // COLS).astype(f32).astype(bf16)

    def masked(s):
        keep = (row >= numbers[col * SLOTS + s]).astype(f32)
        return legendre[s] * keep

    def forward_table(s, carry):
        high, low = split(masked(s))
        fwd_high[s] = dot_t(permt, high).astype(bf16)
        fwd_low[s] = dot_t(permt, low).astype(bf16)
        return carry

    loads[0].wait()
    lax.fori_loop(0, SLOTS, forward_table, 0, unroll=UNROLL)

    def first(sub, carry):
        pltpu.make_async_copy(forcing_in.at[sub], forcing.at[sub], load_sem.at[sub]).wait()

        @pl.when(live(sub))
        def _():
            def slot(s, top):
                high, low = split(in_order(forcing[sub, s]))
                four = dot3(fwd_high[s], fwd_low[s], high, low, dot_t)
                for q in range(SLOTS):
                    spread(four[q * COLS:(q + 1) * COLS], q * SLOTS + s, COLS)
                return jnp.maximum(top, peak(four))

            encode(lax.fori_loop(0, SLOTS, slot, jnp.zeros((1, 128), f32), unroll=UNROLL), sub)

            @pl.when(sub == jnp.where(win > 0, 0, 1))
            def _():
                pl.semaphore_wait(barrier, COLS - 1 + jnp.where(win > 0, 1, 0) + jnp.where(win < 3, 1, 0))

            @pl.when(jnp.logical_and(win > 0, sub == 1))
            def _():
                forward(0)

            start(sub)
            follow(sub, sub)

        return carry

    lax.fori_loop(0, 2, first, 0)

    def inverse_table(s, carry):
        high, low = split(masked(s) * weights[...])
        inv_high[s] = dot(high, perm[...]).astype(bf16)
        inv_low[s] = dot(low, perm[...]).astype(bf16)
        return carry

    lax.fori_loop(0, SLOTS, inverse_table, 0, unroll=UNROLL)

    mix_pad[...] = jnp.zeros((SIZE, SIZE), f32)
    mix_pad[:LEVELS, :LEVELS] = mixing[...]
    high, low = split(mix_pad[...])
    mix_high[...] = high
    mix_low[...] = low

    damp_t = jnp.transpose(jnp.concatenate([damping[...], damping[128:]], axis=0))
    damp[...] = jnp.concatenate([damp_t[:, :128], damp_t[:, :128], damp_t[:, 128:]], axis=1)

    wave = jnp.broadcast_to(row_numbers[...].astype(f32).astype(bf16), (16, SIZE))
    wave = dot(wave, perm[...])[:1]

    def table(q, carry):
        count = points[col * SLOTS + q]
        count_f = jnp.full((1, SIZE), count, jnp.int32).astype(f32)
        part_of = 1.0 / count_f

        def angles(rows, step):
            j = (step * lax.broadcasted_iota(jnp.int32, (rows, SIZE), 0)).astype(f32)
            product = j * wave
            rest = product - jnp.floor(product * part_of) * count_f
            rest = jnp.where(rest < 0.0, rest + count_f, rest)
            rest = jnp.where(rest >= count_f, rest - count_f, rest)
            angle = (2.0 * math.pi) * rest / count_f
            return jnp.cos(angle), jnp.sin(angle)

        cos_a, sin_a = angles(WIDTH // 16, 16)
        cos_b, sin_b = angles(16, 1)
        near = lax.broadcasted_iota(jnp.int32, (16, SIZE), 0)
        for a in range(WIDTH // 16):
            keep = (near + 16 * a < count).astype(f32)
            ca, sa = cos_a[a:a + 1] , sin_a[a:a + 1]
            cos = (ca * cos_b - sa * sin_b) * keep
            sin = (sa * cos_b + ca * sin_b) * keep
            for r, value in ((0, cos), (1, -sin)):
                high, low = split(value)
                tabt_high[q, a * 16:(a + 1) * 16, r * SIZE:(r + 1) * SIZE] = high
                tabt_low[q, a * 16:(a + 1) * 16, r * SIZE:(r + 1) * SIZE] = low
        for r in range(2):
            cut = slice(r * SIZE, (r + 1) * SIZE)
            tab_high[q, cut, :] = dot_t(eye[...], tabt_high[q, :, cut]).astype(bf16)
            tab_low[q, cut, :] = dot_t(eye[...], tabt_low[q, :, cut]).astype(bf16)
        for sub in range(2):
            padded = jnp.concatenate([coefs[sub, q], jnp.zeros((SIZE - LEVELS, WIDTH), bf16)], axis=0)
            for h in range(2):
                cut = slice(h * SIZE, (h + 1) * SIZE)
                coef_t[sub, q, cut, :] = dot_t(eye[...], padded[:, cut]).astype(bf16)
        return carry

    loads[3].wait()
    lax.fori_loop(0, SLOTS, table, 0)

    def write(index, s, result):
        flat = jnp.transpose(result)
        for r in range(2):
            out[index, s, r, :128] = forcing[index, s, r, :128] - flat[r * 128:(r + 1) * 128]
            out[index, s, r, 128:] = forcing[index, s, r, 128:] - flat[256 + r * 64:256 + (r + 1) * 64]
        pltpu.make_async_copy(out.at[index, s], out_in.at[index, s], store_sem.at[index]).start()

    def far_results():
        @pl.when(win < 3)
        def _():
            pltpu.make_async_copy(passed_scale, passed_scale, pass_sem.at[1]).wait()
            pltpu.make_async_copy(passed, passed, pass_sem.at[3]).wait()
            decode(
                lambda d, part: passed[d, :, part * 128:(part + 1) * 128],
                lambda d: passed_scale[...],
            )

            def far_result(s, carry):
                rows = pl.ds(pl.multiple_of(s * SIZE, SIZE), SIZE)
                write(1, s, jnp.concatenate([stage[part, rows, :] for part in range(PARTS)], axis=1))
                return carry

            lax.fori_loop(0, SLOTS, far_result, 0)

        @pl.when(win == 3)
        def _():
            pltpu.make_async_copy(forcing.at[1], out_in.at[1], store_sem.at[1]).start()

    def grid(sub, step):
        arrive(sub, jnp.where(sub == 0, 1, 2))
        if step > 0:
            sent(2 + sub)

        def latitude(q, carry):
            for s in range(SLOTS):
                at = q * SLOTS + s
                last = gathered(at, 2)
                real = jnp.concatenate([gathered(at, 0), last], axis=1)
                imag = jnp.concatenate([gathered(at, 1), pltpu.roll(last, 64, 1)], axis=1)
                for r, value in ((0, real), (1, imag)):
                    high, low = split(value)
                    rows = slice(r * SIZE + s * COLS, r * SIZE + (s + 1) * COLS)
                    op_high[q, rows, :] = high
                    op_low[q, rows, :] = low
            return carry

        lax.fori_loop(0, SLOTS, latitude, 0, unroll=UNROLL)

        def latitude(q, top):
            values = dot3(tabt_high[q], tabt_low[q], op_high[q], op_low[q])
            high, low = split(values)
            mixed = dot3(high, low, mix_high[...], mix_low[...])
            high, low = split(mixed * coef_t[sub, q].astype(f32))
            back = dot3(tab_high[q], tab_low[q], high, low)
            for s in range(SLOTS):
                real = back[s * COLS:(s + 1) * COLS]
                imag = back[SIZE + s * COLS:SIZE + (s + 1) * COLS]
                last = real[:, 128:] + pltpu.roll(imag[:, 128:], 64, 1)
                values = jnp.concatenate([real[:, :128], imag[:, :128], last], axis=1)
                spread(values, q * SLOTS + s, COLS)
                top = jnp.maximum(top, peak(values))
            return top

        encode(lax.fori_loop(0, SLOTS, latitude, jnp.zeros((1, 128), f32), unroll=UNROLL), 2 + sub)
        settle(sub)
        start(2 + sub)
        follow(sub, 2 + sub)

    def spectral(sub, step):
        last = step == STEPS - 1
        if last:
            @pl.when(sub == 1)
            def _():
                far_results()

        arrive(2 + sub, jnp.where(sub == 0, 3, 0), jnp.logical_or(not last, sub == 0))
        sent(sub)

        def operands(s, carry):
            for q in range(SLOTS):
                values = jnp.concatenate([gathered(q * SLOTS + s, part) for part in range(PARTS)], axis=1)
                high, low = split(values)
                rows = slice(q * COLS, (q + 1) * COLS)
                for half, value in ((op_high, high), (op_low, low)):
                    half[s, rows, :] = value[:, :SIZE]
                    half[s, SIZE + q * COLS:SIZE + (q + 1) * COLS, :128] = value[:, SIZE:]
            return carry

        lax.fori_loop(0, SLOTS, operands, 0, unroll=UNROLL)

        def slot(s, top):
            cut = slice(SIZE, 2 * SIZE)
            inc = jnp.concatenate([
                dot3(inv_high[s], inv_low[s], op_high[s, :SIZE], op_low[s, :SIZE]),
                dot3(inv_high[s], inv_low[s], op_high[s, cut, :128], op_low[s, cut, :128]),
            ], axis=1)
            if step == 0:
                before = jnp.transpose(in_order(forcing[sub, s]))
            else:
                before = state[sub, s]
            after = damp[...] * before + inc
            if not last:
                state[sub, s] = after
                high, low = split(after)
                four = dot3(fwd_high[s], fwd_low[s], high, low)
                for q in range(SLOTS):
                    spread(four[q * COLS:(q + 1) * COLS], q * SLOTS + s, COLS)
                return jnp.maximum(top, peak(four))
            state[sub, s] = after
            return jnp.maximum(top, peak(after))

        top = lax.fori_loop(0, SLOTS, slot, jnp.zeros((1, 128), f32), unroll=UNROLL)
        if not last:
            encode(top, sub)
            settle(2 + sub)
            start(sub)
            follow(sub, sub)
        else:
            sent(2 + sub)
            settle(2 + sub)

            @pl.when(sub == 0)
            def _():
                for s in range(SLOTS):
                    for part in range(PARTS):
                        stage[part, s * SIZE:(s + 1) * SIZE, :] = state[0, s, :, part * 128:(part + 1) * 128]
                encode(top, 0)
                pltpu.make_async_remote_copy(
                    src_ref=send_scale.at[0], dst_ref=passed_scale,
                    send_sem=pass_sem.at[0], recv_sem=pass_sem.at[1],
                    device_id=(win - 1, col), device_id_type=MESH,
                ).start()
                pltpu.make_async_remote_copy(
                    src_ref=send.at[0], dst_ref=passed,
                    send_sem=pass_sem.at[2], recv_sem=pass_sem.at[3],
                    device_id=(win - 1, col), device_id_type=MESH,
                ).start()

    for step in range(STEPS):
        for phase in (grid, spectral):
            def both(sub, carry):
                @pl.when(live(sub))
                def _():
                    phase(sub, step)

                return carry

            lax.fori_loop(0, 2, both, 0)

    def near_result(s, carry):
        write(0, s, state[1, s])
        return carry

    lax.fori_loop(0, SLOTS, near_result, 0)

    @pl.when(win > 0)
    def _():
        pltpu.make_async_copy(send_scale.at[0], send_scale.at[0], pass_sem.at[0]).wait()
        pltpu.make_async_copy(send.at[0], send.at[0], pass_sem.at[2]).wait()

    for index in range(2):
        pltpu.make_async_copy(out.at[index], out_in.at[index], store_sem.at[index]).wait()


def shards(forcing, coefficients, legendre, weights, damping, mixing, points, wavenumbers):
    vmem = pl.BlockSpec(memory_space=pltpu.VMEM)
    smem = pl.BlockSpec(memory_space=pltpu.SMEM)
    dma = pltpu.SemaphoreType.DMA
    return pl.pallas_call(
        kernel,
        out_shape=jax.ShapeDtypeStruct(forcing.shape, f32),
        in_specs=[pl.BlockSpec(memory_space=pl.ANY)] * 3 + [vmem] * 4 + [smem] * 2,
        out_specs=pl.BlockSpec(memory_space=pl.ANY),
        scratch_shapes=[
            pltpu.VMEM(forcing.shape, f32),
            pltpu.VMEM(coefficients.shape, bf16),
            pltpu.VMEM(legendre.shape, f32),
            pltpu.VMEM(forcing.shape, f32),
            pltpu.VMEM((4, COLS, ROWS, LANES), jnp.int16),
            pltpu.VMEM((4, COLS, ROWS, LANES), jnp.int16),
            pltpu.VMEM((4, 1, 128), f32),
            pltpu.VMEM((4, COLS, 1, 128), f32),
            pltpu.VMEM((4, RELAYED, ROWS, LANES), jnp.int16),
            pltpu.VMEM((COLS, ROWS, LANES), jnp.int16),
            pltpu.VMEM((1, 128), f32),
            pltpu.VMEM((PARTS, COLS * ROWS, 128), f32),
            pltpu.VMEM((2, SLOTS, SIZE, LANES), f32),
            pltpu.VMEM((SLOTS, SIZE, SIZE), bf16),
            pltpu.VMEM((SLOTS, SIZE, SIZE), bf16),
            pltpu.VMEM((SLOTS, SIZE, SIZE), bf16),
            pltpu.VMEM((SLOTS, SIZE, SIZE), bf16),
            pltpu.VMEM((SIZE, LANES), f32),
            pltpu.VMEM((SIZE, SIZE), f32),
            pltpu.VMEM((SIZE, SIZE), bf16),
            pltpu.VMEM((SIZE, SIZE), bf16),
            pltpu.VMEM((SIZE, SIZE), bf16),
            pltpu.VMEM((SIZE, SIZE), bf16),
            pltpu.VMEM((SLOTS, WIDTH, WIDTH), bf16),
            pltpu.VMEM((SLOTS, WIDTH, WIDTH), bf16),
            pltpu.VMEM((SLOTS, WIDTH, WIDTH), bf16),
            pltpu.VMEM((SLOTS, WIDTH, WIDTH), bf16),
            pltpu.VMEM((2, SLOTS, WIDTH, SIZE), bf16),
            pltpu.VMEM((SLOTS, WIDTH, SIZE), bf16),
            pltpu.VMEM((SLOTS, WIDTH, SIZE), bf16),
            dma((4,)), dma((4,)), dma((4,)), dma((4,)),
            dma((4,)), dma((4,)), dma((4,)), dma((4,)), dma((4,)), dma((4,)), dma((2,)),
        ],
        compiler_params=pltpu.CompilerParams(
            collective_id=0, has_side_effects=True, vmem_limit_bytes=56 * 2**20
        ),
        name="adjoint",
    )(
        forcing, coefficients, legendre, weights.reshape(1, SIZE), damping, mixing,
        wavenumbers.reshape(1, SIZE), points, wavenumbers,
    )


def solution(mesh):
    in_specs = (
        P("win", "col", None, None, None),
        P("win", "col", None, None),
        P("col", None, None),
        P(),
        P(),
        P(),
        P(),
        P(),
    )
    out_specs = P("win", "col", None, None, None)
    return jax.shard_map(shards, mesh=mesh, in_specs=in_specs, out_specs=out_specs, check_vma=False)
```
